512 devices in a mesh: sp: 128 (over y, z_lo, x, core), dp: 4 (over z_hi).
Axes of the slice: x: 4, y: 8, z: 8 (z_hi: 4, z_lo: 2; z = z_hi * 2 + z_lo), core: 2. Of those that a mesh axis runs over, the one named last changes fastest.
Arguments:
- queries: bfloat16 [32768, 5120], P(('sp', 'dp')), may hold values from -60 to 60
- keys: bfloat16 [32768, 1024], P(('sp', 'dp')), may hold values from -60 to 60
- values: bfloat16 [32768, 1024], P(('sp', 'dp')), may hold values from -6 to 6
- lengths: int32 [48], replicated, may hold values from 1 to 3840, 32768 in all
Outputs:
- attended: bfloat16 [32768, 5120], P(('sp', 'dp'))
The draws below stay inside these ranges and needn't reach their ends.
Inputs may be any that keep to these rules, and one draw needn't show every extreme that they name: The lengths sum to 32768; the longest is exactly 3840.
All inputs are finite; a program needn't handle non-finite values.
Results may differ from the reference program's by a relative error of at most 0.0047.
Values may be sent and summed in bfloat16 or wider, within the bound.
No kernel may reach another device: no remote copies, remote signals or barrier semaphores. Data moves between devices by JAX's collectives and lax.ppermute only.
A program may use at most 64 MiB of HBM per device.

```python
import math
import jax
import jax.numpy as jnp
import numpy as np
from jax import lax

QUERY_HEADS = 40
KEY_VALUE_HEADS = 8
HEAD_SIZE = 128
TOK_DEV = 256
SEQS = 48
SPAN = 15
MAXLEN = 3840
PACKED_TOKENS = 32768


def draw_queries(key, part):
    key = jax.random.fold_in(key, 11)
    local_part = jax.random.normal(key, (PACKED_TOKENS, QUERY_HEADS * HEAD_SIZE), jnp.float32)
    return jnp.clip(local_part, -6.0, 6.0).astype(jnp.bfloat16)


def draw_keys(key, part):
    key = jax.random.fold_in(key, 23)
    local_part = jax.random.normal(key, (PACKED_TOKENS, KEY_VALUE_HEADS * HEAD_SIZE), jnp.float32)
    return jnp.clip(local_part, -6.0, 6.0).astype(jnp.bfloat16)


def level_of(key, dims, cuts, low, top_value):
    loudness, own = 1.0, jax.random.fold_in(key, 6)
    for position, blocks in cuts:
        draws = jnp.exp(jax.random.uniform(jax.random.fold_in(own, position), (blocks,), jnp.float32, low / len(cuts), top_value / len(cuts)))
        loudness = loudness * jnp.repeat(draws, dims[position] // blocks).reshape([-1 if axis == position else 1 for axis in range(len(dims))])
    return loudness


def profile(amount, total, bound, slope):
    weights = [(1 << 20) // math.isqrt(rank ** slope) + 1 for rank in range(2, amount + 1)]
    rest, holding = total - bound - (amount - 1), [1] * (amount - 1)
    while rest > 0:
        free = [i for i in range(amount - 1) if holding[i] < bound]
        whole, remaining = sum([weights[i] for i in free]), rest
        for i in free:
            extra = min(bound - holding[i], max(1, remaining * weights[i] // whole), rest)
            holding[i] = holding[i] + extra
            rest = rest - extra
    return np.array([bound] + holding)


def uneven(stream_key, count, total, reach, slope):
    if count == 2:
        one = jax.random.randint(stream_key, (), max(1, total - reach), min(reach, total - 1) + 1)
        return jnp.stack([one, total - one])
    sizes = jnp.asarray(profile(count, total, reach, slope), jnp.int32)
    couples = (count - 1) // 2
    donor, receiver = sizes[1:1 + 2 * couples:2], sizes[2:2 + 2 * couples:2]
    margin = jnp.minimum(donor - 1, reach - receiver)
    passed = jax.random.randint(jax.random.fold_in(stream_key, 1), (couples,), 0, 1 << 20) % (margin + 1)
    sizes = sizes.at[1:1 + 2 * couples:2].set(donor - passed).at[2:2 + 2 * couples:2].set(receiver + passed)
    return sizes[jax.random.permutation(jax.random.fold_in(stream_key, 2), count)]


def centred(stream_key, dims, deviation, bound, shards=(), kind=jnp.bfloat16):
    entries = deviation * jax.random.normal(stream_key, dims, jnp.float32)
    if shards:
        entries = entries * level_of(stream_key, dims, shards, -0.22, 0.18)
    return jnp.clip(entries, -bound, bound).astype(kind)


def setup_inputs(seed: int = 0) -> dict:
    seeds = jax.random.split(jax.random.key(seed), 5)
    return {
        "queries": draw_queries(jax.random.fold_in(seeds[4], 71), 0),
        "keys": draw_keys(jax.random.fold_in(seeds[4], 71), 0),
        "values": centred(seeds[2], (PACKED_TOKENS, KEY_VALUE_HEADS * HEAD_SIZE), 1.0, 6.0, ((0, 512),)),
        "lengths": uneven(seeds[3], SEQS, PACKED_TOKENS, MAXLEN, 2).astype(jnp.int32),
    }


def reference(queries, keys, values, lengths):
    rows_per_block = TOK_DEV
    reachable_rows = SPAN * rows_per_block
    heads_per_group = QUERY_HEADS // KEY_VALUE_HEADS
    doc_ends = jnp.cumsum(lengths).astype(jnp.int32)
    keys_padded = jnp.concatenate([jnp.zeros((reachable_rows, KEY_VALUE_HEADS * HEAD_SIZE), jnp.bfloat16), keys], 0)
    values_padded = jnp.concatenate([jnp.zeros((reachable_rows, KEY_VALUE_HEADS * HEAD_SIZE), jnp.bfloat16), values], 0)
    scaling = 1.0 / math.sqrt(HEAD_SIZE)

    def one_block(block_index):
        first_row = (block_index * rows_per_block).astype(jnp.int32)
        query_block = lax.dynamic_slice_in_dim(queries, first_row, rows_per_block, 0).astype(jnp.float32)
        query_block = query_block.reshape(rows_per_block, KEY_VALUE_HEADS, heads_per_group, HEAD_SIZE)
        key_block = lax.dynamic_slice_in_dim(keys_padded, first_row, reachable_rows + rows_per_block, 0).astype(jnp.float32)
        key_block = key_block.reshape(reachable_rows + rows_per_block, KEY_VALUE_HEADS, HEAD_SIZE)
        value_block = lax.dynamic_slice_in_dim(values_padded, first_row, reachable_rows + rows_per_block, 0).astype(jnp.float32)
        value_block = value_block.reshape(reachable_rows + rows_per_block, KEY_VALUE_HEADS, HEAD_SIZE)
        query_pos = first_row + jnp.arange(rows_per_block, dtype=jnp.int32)
        key_pos = first_row - reachable_rows + jnp.arange(reachable_rows + rows_per_block, dtype=jnp.int32)
        query_doc = lax.optimization_barrier(jnp.sum((doc_ends[None, :] <= query_pos[:, None]).astype(jnp.int32), 1))
        key_doc = lax.optimization_barrier(jnp.sum((doc_ends[None, :] <= key_pos[:, None]).astype(jnp.int32), 1))
        allowed = (key_pos[None, :] <= query_pos[:, None]) & (key_pos[None, :] >= 0) & (key_doc[None, :] == query_doc[:, None])
        scores = jnp.einsum('qhgd,khd->hgqk', query_block, key_block) * scaling
        scores = jnp.where(allowed[None, None], scores, -jnp.inf)
        row_max = lax.optimization_barrier(jnp.max(scores, -1, keepdims=True))
        raw_weights = jnp.exp(scores - row_max)
        weights = (raw_weights / lax.optimization_barrier(jnp.sum(raw_weights, -1, keepdims=True))).astype(jnp.bfloat16)
        result = jnp.einsum('hgqk,khd->qhgd', weights.astype(jnp.float32), value_block)
        return result.reshape(rows_per_block, QUERY_HEADS * HEAD_SIZE).astype(jnp.bfloat16)
    blocks = lax.map(one_block, jnp.arange(PACKED_TOKENS // rows_per_block, dtype=jnp.int32))
    return blocks.reshape(PACKED_TOKENS, QUERY_HEADS * HEAD_SIZE)
```

```python
import functools
import math

import jax
import jax.numpy as jnp
from jax import lax
from jax.experimental import pallas as pl
from jax.experimental.pallas import tpu as pltpu
from jax.sharding import Mesh, PartitionSpec as P

HEAD = 128
HEADS = 40
GROUPS = 8
PER_GROUP = HEADS // GROUPS
TILE = 256
BACK = 4
TILES = 2 * (BACK + 1)
SUPER = 1024
SCALE = math.log2(math.e) / math.sqrt(HEAD)
LOWEST = -1e30


def attend(scalars, q_ref, lows_ref, own_refs, other_refs, out_ref, kt_s, v_s, m_s, acc_s):
    for source, refs in enumerate((own_refs, other_refs)):
        for block, ref in enumerate(refs):
            for half in range(2):
                place = source * TILES + 2 * block + half
                rows = slice(half * TILE, (half + 1) * TILE)
                kt_s[place] = ref[rows, :HEAD].T
                v_s[place, :, :HEAD] = ref[rows, HEAD:]
                v_s[place, :, HEAD:] = jnp.ones((TILE, HEAD), jnp.bfloat16)

    for block in range(2):
        first = scalars[block]
        low_first = scalars[2 + block]
        low_last = scalars[4 + block]
        m_s[...] = jnp.full(m_s.shape, LOWEST, jnp.float32)
        acc_s[...] = jnp.zeros(acc_s.shape, jnp.float32)
        rows = slice(block * TILE, (block + 1) * TILE)

        def visit(place, allowed):
            kt = kt_s[place]
            v = v_s[place]
            for head in range(PER_GROUP):
                q = q_ref[rows, head * HEAD : (head + 1) * HEAD]
                scores = jnp.dot(q, kt, preferred_element_type=jnp.float32) * SCALE
                if allowed is not None:
                    scores = jnp.where(allowed, scores, LOWEST)
                m_old = m_s[head]
                m_new = jnp.maximum(m_old, jnp.max(scores, 1, keepdims=True))
                m_s[head] = m_new
                alpha = jnp.exp2(m_old - m_new)
                weights = jnp.exp2(scores - jnp.concatenate([m_new, m_new], 1)).astype(jnp.bfloat16)
                part = jnp.dot(weights, v, preferred_element_type=jnp.float32)
                acc_s[head] = acc_s[head] * jnp.concatenate([alpha, alpha], 1) + part

        for source in range(2):
            base = scalars[6 + source]
            start = jnp.maximum(0, (low_first - base + 2 * TILE - TILE) // (2 * TILE))
            stop = (first - base) // (2 * TILE) + 1

            def step(tile, _):
                position = base + tile * 2 * TILE
                place = source * TILES + tile
                whole = (position >= low_last) & (position + TILE - 1 <= first)

                @pl.when(whole)
                def _():
                    visit(place, None)

                @pl.when(jnp.logical_not(whole))
                def _():
                    key = position + lax.broadcasted_iota(jnp.int32, (TILE, TILE), 1)
                    query = first + lax.broadcasted_iota(jnp.int32, (TILE, TILE), 0)
                    low = lows_ref[rows, :]
                    low = jnp.concatenate([low, low], 1)
                    visit(place, (key <= query) & (key >= low))

                return 0

            lax.fori_loop(start, stop, step, 0)

        for head in range(PER_GROUP):
            total = acc_s[head]
            out_ref[rows, head * HEAD : (head + 1) * HEAD] = (
                total[:, :HEAD] / total[:, HEAD:]
            ).astype(jnp.bfloat16)


def kernel(scalars, q_ref, lows_ref, *refs):
    own, other = refs[: BACK + 1], refs[BACK + 1 : 2 * (BACK + 1)]
    attend(scalars, q_ref, lows_ref, own, other, *refs[2 * (BACK + 1) :])


def call_kernel(scalars, q, lows, own, other):
    vmem = pl.BlockSpec(memory_space=pltpu.VMEM)
    return pl.pallas_call(
        kernel,
        out_shape=jax.ShapeDtypeStruct(q.shape, jnp.bfloat16),
        in_specs=[pl.BlockSpec(memory_space=pltpu.SMEM)] + [vmem] * (2 + len(own) + len(other)),
        out_specs=vmem,
        scratch_shapes=[
            pltpu.VMEM((2 * TILES, HEAD, TILE), jnp.bfloat16),
            pltpu.VMEM((2 * TILES, TILE, 2 * HEAD), jnp.bfloat16),
            pltpu.VMEM((PER_GROUP, TILE, HEAD), jnp.float32),
            pltpu.VMEM((PER_GROUP, TILE, 2 * HEAD), jnp.float32),
        ],
        compiler_params=pltpu.CompilerParams(vmem_limit_bytes=40 * 1024 * 1024),
        cost_estimate=pl.CostEstimate(
            flops=2 * 2 * 2560 * 4096 * 128, bytes_accessed=8 << 20, transcendentals=2560 * 4096
        ),
        name="attention",
    )(scalars, q, lows, *own, *other)


def bounds(index, core, lengths):
    starts = jnp.cumsum(lengths) - lengths
    firsts = index * SUPER + core * TILE + jnp.arange(2, dtype=jnp.int32) * 2 * TILE
    query = (firsts[:, None] + jnp.arange(TILE, dtype=jnp.int32)[None, :]).reshape(2 * TILE)
    low = jnp.max(jnp.where(starts[None, :] <= query[:, None], starts[None, :], 0), 1)
    lows = jnp.broadcast_to(low[:, None], (2 * TILE, HEAD))
    base = (index - BACK) * SUPER
    bases = jnp.stack([base + core * TILE, base + (1 - core) * TILE])
    scalars = jnp.concatenate([firsts, low[::TILE], low[TILE - 1 :: TILE], bases])
    return scalars.astype(jnp.int32), lows.astype(jnp.int32)


def local(queries, keys, values, lengths):
    rows = keys.shape[0]
    pair = jnp.stack([keys.reshape(rows, GROUPS, HEAD), values.reshape(rows, GROUPS, HEAD)], 2)
    pair = pair.reshape(rows, GROUPS * 2 * HEAD)
    chain = ("y", "w", "X")
    heads = ("l", "d")
    own = lax.all_to_all(pair, heads, split_axis=1, concat_axis=0, tiled=True)
    q = lax.all_to_all(queries, heads, split_axis=1, concat_axis=0, tiled=True)
    length = lax.axis_size("y") * 4
    held = [own]
    for distance in range(1, BACK + 1):
        route = [(i, i + distance) for i in range(length - distance)]
        held.append(lax.ppermute(own, chain, route))
    held = held[::-1]
    swapped = lax.ppermute(jnp.stack(held), "c", [(0, 1), (1, 0)])
    other = [swapped[i] for i in range(BACK + 1)]
    index = lax.axis_index(chain)
    scalars, lows = bounds(index, lax.axis_index("c"), lengths)
    out = call_kernel(scalars, q, lows, held, other)
    return lax.all_to_all(out, heads, split_axis=0, concat_axis=1, tiled=True)


def solution(mesh):
    fine = Mesh(mesh.devices.reshape(8, 2, 2, 2, 2, 4), ("y", "w", "X", "l", "c", "d"))
    rows = P(("y", "w", "X", "l", "c", "d"), None)
    return jax.shard_map(
        local, mesh=fine, in_specs=(rows, rows, rows, P()), out_specs=rows, check_vma=False
    )
```

```python
import functools
import math

import jax
import jax.numpy as jnp
from jax import lax
from jax.experimental import pallas as pl
from jax.experimental.pallas import tpu as pltpu
from jax.sharding import Mesh, PartitionSpec as P

HEAD = 128
HEADS = 40
GROUPS = 8
PER_GROUP = HEADS // GROUPS
PART = 256
TILE = 2 * PART
SUPER = 2 * TILE
ROWS = PER_GROUP * PART
SCALE = math.log2(math.e) / math.sqrt(HEAD)
LOWEST = -1e30


def double(x, times=2):
    return jnp.concatenate([x] * times, 1)


def visit(q, kt, v, m_ref, acc_ref, allowed):
    scores = jnp.dot(q, kt, preferred_element_type=jnp.float32)
    weights, decay = [], []
    for head in range(PER_GROUP):
        rows = slice(head * PART, (head + 1) * PART)
        scaled = scores[rows] * SCALE
        if allowed is not None:
            scaled = jnp.where(allowed, scaled, LOWEST)
        m_old = m_ref[rows]
        m_new = jnp.maximum(m_old, jnp.max(scaled, 1, keepdims=True))
        m_ref[rows] = m_new
        decay.append(jnp.exp2(m_old - m_new))
        weights.append(jnp.exp2(scaled - double(m_new, TILE // HEAD)).astype(jnp.bfloat16))
    part = jnp.dot(jnp.concatenate(weights, 0), v, preferred_element_type=jnp.float32)
    for head in range(PER_GROUP):
        rows = slice(head * PART, (head + 1) * PART)
        acc_ref[rows] = acc_ref[rows] * double(decay[head]) + part[rows]


def load(own_refs, other_refs, kt_s, v_s):
    tile = 0
    for own, other in zip(own_refs, other_refs):
        for half in range(2):
            rows = slice(half * PART, (half + 1) * PART)
            for source, ref in enumerate((own, other)):
                span = slice(source * PART, (source + 1) * PART)
                kt_s[tile, :, span] = ref[rows, :HEAD].T
                v_s[tile, span, :HEAD] = ref[rows, HEAD:]
                v_s[tile, span, HEAD:] = jnp.ones((PART, HEAD), jnp.bfloat16)
            tile += 1


def sweep(scalars, block, slots, q_s, lows_ref, kt_s, v_s, m_ref, acc_ref):
    first = scalars[block]
    low_first = scalars[2 + block]
    low_last = scalars[4 + block]
    core = scalars[6]
    rows = pl.ds(pl.multiple_of(block * PART, PART), PART)
    for place, slot in enumerate(slots):
        base = scalars[7 + slot]
        start = jnp.clip((low_first - base) // TILE, 0, 2)
        stop = jnp.clip((first + PART - 1 - base) // TILE + 1, 0, 2)

        def step(tile, _):
            position = base + tile * TILE
            whole = (position >= low_last) & (position + TILE - 1 <= first)

            def go(allowed):
                kt, v = kt_s[2 * place + tile], v_s[2 * place + tile]
                visit(q_s[block], kt, v, m_ref.at[block], acc_ref.at[block], allowed)

            @pl.when(whole)
            def _():
                go(None)

            @pl.when(jnp.logical_not(whole))
            def _():
                column = lax.broadcasted_iota(jnp.int32, (PART, TILE), 1)
                key = position + jnp.bitwise_xor(column, core * PART)
                query = first + lax.broadcasted_iota(jnp.int32, (PART, TILE), 0)
                low = double(lows_ref[rows, :], TILE // HEAD)
                go((key <= query) & (key >= low))

            return 0

        lax.fori_loop(start, stop, step, 0)


def stack_heads(q_ref, q_s):
    for block in range(2):
        for head in range(PER_GROUP):
            q_s[block, head * PART : (head + 1) * PART] = q_ref[
                block * PART : (block + 1) * PART, head * HEAD : (head + 1) * HEAD
            ]


def fold_kernel(slots, first, last, scalars, q_ref, lows_ref, *refs):
    count = len(slots)
    own, other, refs = refs[0], refs[1], refs[2:]
    if not first:
        m_in, acc_in, refs = refs[0], refs[1], refs[2:]
    if last:
        out_ref, refs = refs[0], refs[1:]
    m_ref, acc_ref, q_s, kt_s, v_s = refs
    stack_heads(q_ref, q_s)
    load([own.at[i] for i in range(count)], [other.at[i] for i in range(count)], kt_s, v_s)
    if first:
        m_ref[...] = jnp.full(m_ref.shape, LOWEST, jnp.float32)
        acc_ref[...] = jnp.zeros(acc_ref.shape, jnp.float32)
    else:
        m_ref[...] = m_in[...]
        acc_ref[...] = acc_in[...]

    def one(block, _):
        sweep(scalars, block, slots, q_s, lows_ref, kt_s, v_s, m_ref, acc_ref)
        if last:
            rows = pl.ds(pl.multiple_of(block * PART, PART), PART)
            for head in range(PER_GROUP):
                total = acc_ref[block, head * PART : (head + 1) * PART]
                out_ref[rows, head * HEAD : (head + 1) * HEAD] = (
                    total[:, :HEAD] / total[:, HEAD:]
                ).astype(jnp.bfloat16)
        return 0

    lax.fori_loop(0, 2, one, 0)


def specs(count):
    return [pl.BlockSpec(memory_space=pltpu.SMEM)] + [pl.BlockSpec(memory_space=pltpu.VMEM)] * count


def scratch(tiles):
    return [
        pltpu.VMEM((2, ROWS, HEAD), jnp.bfloat16),
        pltpu.VMEM((tiles, HEAD, TILE), jnp.bfloat16),
        pltpu.VMEM((tiles, TILE, 2 * HEAD), jnp.bfloat16),
    ]


def cost(tiles):
    pairs = 2 * ROWS * tiles * TILE
    return pl.CostEstimate(flops=4 * HEAD * pairs, bytes_accessed=4 << 20, transcendentals=pairs)


STATE = (
    jax.ShapeDtypeStruct((2, ROWS, HEAD), jnp.float32),
    jax.ShapeDtypeStruct((2, ROWS, 2 * HEAD), jnp.float32),
)
PARAMS = pltpu.CompilerParams(vmem_limit_bytes=32 * 1024 * 1024)


def fold(slots, scalars, q, lows, own, other, state=(), last=False):
    count = len(slots)
    vmem = pl.BlockSpec(memory_space=pltpu.VMEM)
    keep = [pltpu.VMEM(s.shape, s.dtype) for s in STATE] if last else []
    return pl.pallas_call(
        functools.partial(fold_kernel, slots, not state, last),
        out_shape=jax.ShapeDtypeStruct(q.shape, jnp.bfloat16) if last else STATE,
        in_specs=specs(4 + len(state)),
        out_specs=vmem if last else [vmem] * 2,
        scratch_shapes=keep + scratch(2 * count),
        compiler_params=PARAMS,
        cost_estimate=cost(2 * count),
        name="attend_%d" % slots[0],
    )(scalars, q, lows, own, other, *state)


def bounds(index, core, lengths):
    starts = jnp.cumsum(lengths) - lengths
    firsts = index * SUPER + core * PART + jnp.arange(2, dtype=jnp.int32) * TILE
    query = (firsts[:, None] + jnp.arange(PART, dtype=jnp.int32)[None, :]).reshape(TILE)
    low = jnp.max(jnp.where(starts[None, :] <= query[:, None], starts[None, :], 0), 1)
    lows = jnp.broadcast_to(low[:, None], (TILE, HEAD))
    bases = [index, index - 2, index - 4, index - 1, index - 3]
    place = jnp.stack([core] + [base * SUPER for base in bases])
    scalars = jnp.concatenate([firsts, low[::PART], low[PART - 1 :: PART], place])
    return scalars.astype(jnp.int32), lows.astype(jnp.int32)


def forward(block, axes, distance):
    size = math.prod(lax.axis_size(axis) for axis in axes)
    return lax.ppermute(block, axes, [(i, i + distance) for i in range(size - distance)])


def flip(block, axis):
    return lax.ppermute(block, axis, [(0, 1), (1, 0)])


def local(queries, keys, values, lengths):
    rows = keys.shape[0]
    pair = jnp.stack([keys.reshape(rows, GROUPS, HEAD), values.reshape(rows, GROUPS, HEAD)], 2)
    pair = pair.reshape(rows, GROUPS * 2 * HEAD)
    chain = ("y", "w", "X")
    heads = ("l", "d")
    index, core = lax.axis_index(chain), lax.axis_index("c")
    scalars, lows = bounds(index, core, lengths)
    own = lax.all_to_all(pair, heads, split_axis=1, concat_axis=0, tiled=True)
    q = lax.all_to_all(queries, heads, split_axis=1, concat_axis=0, tiled=True)
    near = jnp.stack([own, forward(own, chain, 2), forward(own, chain, 4)])
    send = lax.dynamic_slice_in_dim(near, lax.axis_index("X"), 2, 0)
    distant = flip(send, "X")
    m, acc = fold((0, 1, 2), scalars, q, lows, near, flip(near, "c"))
    distant, m = lax.optimization_barrier((distant, m))
    out = fold((3, 4), scalars, q, lows, distant, flip(distant, "c"), (m, acc), last=True)
    return lax.all_to_all(out, heads, split_axis=0, concat_axis=1, tiled=True)


def solution(mesh):
    fine = Mesh(mesh.devices.reshape(8, 2, 2, 2, 2, 4), ("y", "w", "X", "l", "c", "d"))
    rows = P(("y", "w", "X", "l", "c", "d"), None)
    return jax.shard_map(
        local, mesh=fine, in_specs=(rows, rows, rows, P()), out_specs=rows, check_vma=False
    )
```

```python
import functools
import math

import jax
import jax.numpy as jnp
from jax import lax
from jax.experimental import pallas as pl
from jax.experimental.pallas import tpu as pltpu
from jax.sharding import Mesh, PartitionSpec as P

HEAD = 128
HEADS = 40
GROUPS = 8
PER_GROUP = HEADS // GROUPS
PART = 256
TILE = 2 * PART
SUPER = 2 * TILE
ROWS = PER_GROUP * PART
SCALE = math.log2(math.e) / math.sqrt(HEAD)
LOWEST = -1e30


def double(x, times=2):
    return jnp.concatenate([x] * times, 1)


def visit(q, kt, v, m_ref, acc_ref, allowed):
    scores = jnp.dot(q, kt, preferred_element_type=jnp.float32)
    weights, decay = [], []
    for head in range(PER_GROUP):
        rows = slice(head * PART, (head + 1) * PART)
        raw = scores[rows]
        if allowed is not None:
            raw = jnp.where(allowed, raw, LOWEST)
        m_old = m_ref[rows]
        m_new = jnp.maximum(m_old, jnp.max(raw, 1, keepdims=True))
        m_ref[rows] = m_new
        decay.append(jnp.exp2((m_old - m_new) * SCALE))
        weights.append(jnp.exp2((raw - double(m_new, TILE // HEAD)) * SCALE).astype(jnp.bfloat16))
    part = jnp.dot(jnp.concatenate(weights, 0), v, preferred_element_type=jnp.float32)
    for head in range(PER_GROUP):
        rows = slice(head * PART, (head + 1) * PART)
        acc_ref[rows] = acc_ref[rows] * double(decay[head]) + part[rows]


def halves(own_refs, other_refs):
    tile = 0
    for own, other in zip(own_refs, other_refs):
        for half in range(2):
            rows = slice(half * PART, (half + 1) * PART)
            for source, ref in enumerate((own, other)):
                yield tile, slice(source * PART, (source + 1) * PART), ref, rows
            tile += 1


def load_keys(own_refs, other_refs, kt_s):
    for tile, span, ref, rows in halves(own_refs, other_refs):
        kt_s[tile, :, span] = ref[rows, :HEAD].T


def load_values(own_refs, other_refs, v_s):
    for tile, span, ref, rows in halves(own_refs, other_refs):
        v_s[tile, span, :HEAD] = ref[rows, HEAD:]
        v_s[tile, span, HEAD:] = jnp.ones((PART, HEAD), jnp.bfloat16)


def sweep(scalars, block, sources, q_s, lows_ref, m_ref, acc_ref):
    first = scalars[block]
    low_first = scalars[2 + block]
    low_last = scalars[4 + block]
    core = scalars[6]
    rows = pl.ds(pl.multiple_of(block * PART, PART), PART)
    for slot, kt_s, key_place, v_s, value_place in sources:
        base = scalars[7 + slot]
        start = jnp.clip((low_first - base) // TILE, 0, 2)
        stop = jnp.clip((first + PART - 1 - base) // TILE + 1, 0, 2)

        def step(tile, _):
            position = base + tile * TILE
            whole = (position >= low_last) & (position + TILE - 1 <= first)

            def go(allowed):
                kt, v = kt_s[key_place + tile], v_s[value_place + tile]
                visit(q_s[block], kt, v, m_ref.at[block], acc_ref.at[block], allowed)

            @pl.when(whole)
            def _():
                go(None)

            @pl.when(jnp.logical_not(whole))
            def _():
                column = lax.broadcasted_iota(jnp.int32, (PART, TILE), 1)
                key = position + jnp.bitwise_xor(column, core * PART)
                query = first + lax.broadcasted_iota(jnp.int32, (PART, TILE), 0)
                low = double(lows_ref[rows, :], TILE // HEAD)
                go((key <= query) & (key >= low))

            return 0

        lax.fori_loop(start, stop, step, 0)


def stack_heads(q_ref, q_s):
    for block in range(2):
        for head in range(PER_GROUP):
            q_s[block, head * PART : (head + 1) * PART] = q_ref[
                block * PART : (block + 1) * PART, head * HEAD : (head + 1) * HEAD
            ]


def blocks(ref):
    return [ref.at[i] for i in range(ref.shape[0])]


def ready_kernel(own, other, kt_ref):
    load_keys(blocks(own), blocks(other), kt_ref)


def ready(own, other):
    vmem = pl.BlockSpec(memory_space=pltpu.VMEM)
    return pl.pallas_call(
        ready_kernel,
        out_shape=jax.ShapeDtypeStruct((2 * own.shape[0], HEAD, TILE), jnp.bfloat16),
        in_specs=[vmem] * 2,
        out_specs=vmem,
        compiler_params=PARAMS,
        cost_estimate=cost(8),
        name="ready",
    )(own, other)


def fold_kernel(slots, first, last, scalars, q_ref, lows_ref, *refs):
    if first:
        kt_ref, own, other, own_last, other_last, m_ref, acc_ref, q_s, kt_s, v_s = refs
        load_keys([own_last], [other_last], kt_s)
        load_values(blocks(own) + [own_last], blocks(other) + [other_last], v_s)
        sources = [(slot, kt_ref, 2 * i, v_s, 2 * i) for i, slot in enumerate(slots[:-1])]
        sources.append((slots[-1], kt_s, 0, v_s, 2 * len(sources)))
        m_ref[...] = jnp.full(m_ref.shape, LOWEST, jnp.float32)
        acc_ref[...] = jnp.zeros(acc_ref.shape, jnp.float32)
    else:
        own, other, m_in, acc_in, out_ref, m_ref, acc_ref, q_s, kt_s, v_s = refs
        load_keys(blocks(own), blocks(other), kt_s)
        load_values(blocks(own), blocks(other), v_s)
        sources = [(slot, kt_s, 2 * i, v_s, 2 * i) for i, slot in enumerate(slots)]
        m_ref[...] = m_in[...]
        acc_ref[...] = acc_in[...]
    stack_heads(q_ref, q_s)

    def one(block, _):
        sweep(scalars, block, sources, q_s, lows_ref, m_ref, acc_ref)
        if last:
            rows = pl.ds(pl.multiple_of(block * PART, PART), PART)
            for head in range(PER_GROUP):
                total = acc_ref[block, head * PART : (head + 1) * PART]
                out_ref[rows, head * HEAD : (head + 1) * HEAD] = (
                    total[:, :HEAD] / total[:, HEAD:]
                ).astype(jnp.bfloat16)
        return 0

    lax.fori_loop(0, 2, one, 0)


def specs(count):
    return [pl.BlockSpec(memory_space=pltpu.SMEM)] + [pl.BlockSpec(memory_space=pltpu.VMEM)] * count


def scratch(tiles):
    return [
        pltpu.VMEM((2, ROWS, HEAD), jnp.bfloat16),
        pltpu.VMEM((tiles, HEAD, TILE), jnp.bfloat16),
        pltpu.VMEM((tiles, TILE, 2 * HEAD), jnp.bfloat16),
    ]


def cost(tiles):
    pairs = 2 * ROWS * tiles * TILE
    return pl.CostEstimate(flops=4 * HEAD * pairs, bytes_accessed=4 << 20, transcendentals=pairs)


STATE = (
    jax.ShapeDtypeStruct((2, ROWS, HEAD), jnp.float32),
    jax.ShapeDtypeStruct((2, ROWS, 2 * HEAD), jnp.float32),
)
PARAMS = pltpu.CompilerParams(vmem_limit_bytes=32 * 1024 * 1024)


def fold(slots, scalars, q, lows, keys, state=(), last=False):
    vmem = pl.BlockSpec(memory_space=pltpu.VMEM)
    keep = [pltpu.VMEM(s.shape, s.dtype) for s in STATE] if last else []
    return pl.pallas_call(
        functools.partial(fold_kernel, slots, not state, last),
        out_shape=jax.ShapeDtypeStruct(q.shape, jnp.bfloat16) if last else STATE,
        in_specs=specs(2 + len(keys) + len(state)),
        out_specs=vmem if last else [vmem] * 2,
        scratch_shapes=keep + scratch(2 * len(slots)),
        compiler_params=PARAMS,
        cost_estimate=cost(2 * len(slots)),
        name="attend_%d" % slots[0],
    )(scalars, q, lows, *keys, *state)


def bounds(index, core, lengths):
    starts = jnp.cumsum(lengths) - lengths
    firsts = index * SUPER + core * PART + jnp.arange(2, dtype=jnp.int32) * TILE
    query = (firsts[:, None] + jnp.arange(PART, dtype=jnp.int32)[None, :]).reshape(TILE)
    low = jnp.max(jnp.where(starts[None, :] <= query[:, None], starts[None, :], 0), 1)
    lows = jnp.broadcast_to(low[:, None], (TILE, HEAD))
    bases = [index, index - 2, index - 4, index - 1, index - 3]
    place = jnp.stack([core] + [base * SUPER for base in bases])
    scalars = jnp.concatenate([firsts, low[::PART], low[PART - 1 :: PART], place])
    return scalars.astype(jnp.int32), lows.astype(jnp.int32)


def forward(block, axes, distance):
    size = math.prod(lax.axis_size(axis) for axis in axes)
    return lax.ppermute(block, axes, [(i, i + distance) for i in range(size - distance)])


def flip(block, axis):
    return lax.ppermute(block, axis, [(0, 1), (1, 0)])


def local(queries, keys, values, lengths):
    rows = keys.shape[0]
    pair = jnp.stack([keys.reshape(rows, GROUPS, HEAD), values.reshape(rows, GROUPS, HEAD)], 2)
    pair = pair.reshape(rows, GROUPS * 2 * HEAD)
    chain = ("y", "w", "X")
    heads = ("l", "d")
    index, core = lax.axis_index(chain), lax.axis_index("c")
    scalars, lows = bounds(index, core, lengths)
    own = lax.all_to_all(pair, heads, split_axis=1, concat_axis=0, tiled=True)
    q = lax.all_to_all(queries, heads, split_axis=1, concat_axis=0, tiled=True)
    two = forward(own, chain, 2)
    four = forward(own, chain, 4)
    near = jnp.stack([own, two])
    left = lax.axis_index("X") == 0
    mine, nearby, farther = lax.optimization_barrier((own, two, four))
    send = jnp.stack([jnp.where(left, mine, nearby), jnp.where(left, nearby, farther)])
    distant = flip(send, "X")
    near_other = flip(near, "c")
    keys = [ready(near, near_other), near, near_other, four, flip(four, "c")]
    m, acc = fold((0, 1, 2), scalars, q, lows, keys)
    distant, m = lax.optimization_barrier((distant, m))
    keys = [distant, flip(distant, "c")]
    out = fold((3, 4), scalars, q, lows, keys, (m, acc), last=True)
    return lax.all_to_all(out, heads, split_axis=0, concat_axis=1, tiled=True)


def solution(mesh):
    fine = Mesh(mesh.devices.reshape(8, 2, 2, 2, 2, 4), ("y", "w", "X", "l", "c", "d"))
    rows = P(("y", "w", "X", "l", "c", "d"), None)
    return jax.shard_map(
        local, mesh=fine, in_specs=(rows, rows, rows, P()), out_specs=rows, check_vma=False
    )
```

```python
import functools
import math

import jax
import jax.numpy as jnp
from jax import lax
from jax.experimental import pallas as pl
from jax.experimental.pallas import tpu as pltpu
from jax.sharding import Mesh, PartitionSpec as P

HEAD = 128
HEADS = 40
GROUPS = 8
PER_GROUP = HEADS // GROUPS
PART = 256
TILE = 2 * PART
SUPER = 2 * TILE
ROWS = PER_GROUP * PART
SCALE = math.log2(math.e) / math.sqrt(HEAD)
LOWEST = -1e30


def double(x, times=2):
    return jnp.concatenate([x] * times, 1)


def visit(q, kt, v, m_ref, acc_ref, allowed):
    scores = jnp.dot(q, kt, preferred_element_type=jnp.float32)
    weights, decay = [], []
    for head in range(PER_GROUP):
        rows = slice(head * PART, (head + 1) * PART)
        raw = scores[rows]
        if allowed is not None:
            raw = jnp.where(allowed, raw, LOWEST)
        m_old = m_ref[rows]
        m_new = jnp.maximum(m_old, jnp.max(raw, 1, keepdims=True))
        m_ref[rows] = m_new
        decay.append(jnp.exp2((m_old - m_new) * SCALE))
        weights.append(jnp.exp2((raw - double(m_new, TILE // HEAD)) * SCALE).astype(jnp.bfloat16))
    part = jnp.dot(jnp.concatenate(weights, 0), v, preferred_element_type=jnp.float32)
    for head in range(PER_GROUP):
        rows = slice(head * PART, (head + 1) * PART)
        acc_ref[rows] = acc_ref[rows] * double(decay[head]) + part[rows]


def halves(own_refs, other_refs):
    tile = 0
    for own, other in zip(own_refs, other_refs):
        for half in range(2):
            rows = slice(half * PART, (half + 1) * PART)
            for source, ref in enumerate((own, other)):
                yield tile, slice(source * PART, (source + 1) * PART), ref, rows
            tile += 1


def load_keys(own_refs, other_refs, kt_s):
    for tile, span, ref, rows in halves(own_refs, other_refs):
        kt_s[tile, :, span] = ref[rows, :HEAD].T


def load_values(own_refs, other_refs, v_s):
    for tile, span, ref, rows in halves(own_refs, other_refs):
        v_s[tile, span, :HEAD] = ref[rows, HEAD:]
        v_s[tile, span, HEAD:] = jnp.ones((PART, HEAD), jnp.bfloat16)


def sweep(scalars, block, sources, q_s, lows_ref, m_ref, acc_ref):
    first = scalars[block]
    low_first = scalars[2 + block]
    low_last = scalars[4 + block]
    core = scalars[6]
    rows = pl.ds(pl.multiple_of(block * PART, PART), PART)
    for slot, kt_s, key_place, v_s, value_place in sources:
        base = scalars[7 + slot]
        start = jnp.clip((low_first - base) // TILE, 0, 2)
        stop = jnp.clip((first + PART - 1 - base) // TILE + 1, 0, 2)

        def step(tile, _):
            position = base + tile * TILE
            whole = (position >= low_last) & (position + TILE - 1 <= first)

            def go(allowed):
                kt, v = kt_s[key_place + tile], v_s[value_place + tile]
                visit(q_s[block], kt, v, m_ref.at[block], acc_ref.at[block], allowed)

            @pl.when(whole)
            def _():
                go(None)

            @pl.when(jnp.logical_not(whole))
            def _():
                column = lax.broadcasted_iota(jnp.int32, (PART, TILE), 1)
                key = position + jnp.bitwise_xor(column, core * PART)
                query = first + lax.broadcasted_iota(jnp.int32, (PART, TILE), 0)
                low = double(lows_ref[rows, :], TILE // HEAD)
                go((key <= query) & (key >= low))

            return 0

        lax.fori_loop(start, stop, step, 0)


def stack_heads(q_ref, q_s):
    for block in range(2):
        for head in range(PER_GROUP):
            q_s[block, head * PART : (head + 1) * PART] = q_ref[
                block * PART : (block + 1) * PART, head * HEAD : (head + 1) * HEAD
            ]


def blocks(ref):
    return [ref.at[i] for i in range(ref.shape[0])]


def ready_kernel(own, other, kt_ref):
    load_keys(blocks(own), blocks(other), kt_ref)


def ready(own, other):
    vmem = pl.BlockSpec(memory_space=pltpu.VMEM)
    return pl.pallas_call(
        ready_kernel,
        out_shape=jax.ShapeDtypeStruct((2 * own.shape[0], HEAD, TILE), jnp.bfloat16),
        in_specs=[vmem] * 2,
        out_specs=vmem,
        compiler_params=PARAMS,
        cost_estimate=cost(4),
        name="ready",
    )(own, other)


def fold_kernel(slots, first, last, scalars, q_ref, lows_ref, *refs):
    if first:
        kt_ref, own, other, m_ref, acc_ref, q_s, v_s = refs
        load_values(blocks(own), blocks(other), v_s)
        sources = [(slot, kt_ref, 2 * i, v_s, 2 * i) for i, slot in enumerate(slots)]
        m_ref[...] = jnp.full(m_ref.shape, LOWEST, jnp.float32)
        acc_ref[...] = jnp.zeros(acc_ref.shape, jnp.float32)
    else:
        own, other, m_in, acc_in, out_ref, m_ref, acc_ref, q_s, kt_s, v_s = refs
        load_keys(blocks(own), blocks(other), kt_s)
        load_values(blocks(own), blocks(other), v_s)
        sources = [(slot, kt_s, 2 * i, v_s, 2 * i) for i, slot in enumerate(slots)]
        m_ref[...] = m_in[...]
        acc_ref[...] = acc_in[...]
    stack_heads(q_ref, q_s)

    def one(block, _):
        sweep(scalars, block, sources, q_s, lows_ref, m_ref, acc_ref)
        if last:
            rows = pl.ds(pl.multiple_of(block * PART, PART), PART)
            for head in range(PER_GROUP):
                total = acc_ref[block, head * PART : (head + 1) * PART]
                out_ref[rows, head * HEAD : (head + 1) * HEAD] = (
                    total[:, :HEAD] / total[:, HEAD:]
                ).astype(jnp.bfloat16)
        return 0

    lax.fori_loop(0, 2, one, 0)


def specs(count):
    return [pl.BlockSpec(memory_space=pltpu.SMEM)] + [pl.BlockSpec(memory_space=pltpu.VMEM)] * count


def scratch(tiles):
    return [
        pltpu.VMEM((2, ROWS, HEAD), jnp.bfloat16),
        pltpu.VMEM((tiles, HEAD, TILE), jnp.bfloat16),
        pltpu.VMEM((tiles, TILE, 2 * HEAD), jnp.bfloat16),
    ]


def cost(tiles):
    pairs = 2 * ROWS * tiles * TILE
    return pl.CostEstimate(flops=4 * HEAD * pairs, bytes_accessed=4 << 20, transcendentals=pairs)


STATE = (
    jax.ShapeDtypeStruct((2, ROWS, HEAD), jnp.float32),
    jax.ShapeDtypeStruct((2, ROWS, 2 * HEAD), jnp.float32),
)
PARAMS = pltpu.CompilerParams(vmem_limit_bytes=32 * 1024 * 1024)


def fold(slots, scalars, q, lows, keys, state=(), last=False):
    vmem = pl.BlockSpec(memory_space=pltpu.VMEM)
    keep = [pltpu.VMEM(s.shape, s.dtype) for s in STATE] if last else []
    return pl.pallas_call(
        functools.partial(fold_kernel, slots, not state, last),
        out_shape=jax.ShapeDtypeStruct(q.shape, jnp.bfloat16) if last else STATE,
        in_specs=specs(2 + len(keys) + len(state)),
        out_specs=vmem if last else [vmem] * 2,
        scratch_shapes=keep + (scratch(2 * len(slots)) if last else scratch(2 * len(slots))[::2]),
        compiler_params=PARAMS,
        cost_estimate=cost(2 * len(slots)),
        name="attend_%d" % slots[0],
    )(scalars, q, lows, *keys, *state)


def bounds(index, core, lengths):
    starts = jnp.cumsum(lengths) - lengths
    firsts = index * SUPER + core * PART + jnp.arange(2, dtype=jnp.int32) * TILE
    query = (firsts[:, None] + jnp.arange(PART, dtype=jnp.int32)[None, :]).reshape(TILE)
    low = jnp.max(jnp.where(starts[None, :] <= query[:, None], starts[None, :], 0), 1)
    lows = jnp.broadcast_to(low[:, None], (TILE, HEAD))
    bases = [index, index - 2, index - 4, index - 1, index - 3]
    place = jnp.stack([core] + [base * SUPER for base in bases])
    scalars = jnp.concatenate([firsts, low[::PART], low[PART - 1 :: PART], place])
    return scalars.astype(jnp.int32), lows.astype(jnp.int32)


def forward(block, axes, distance):
    size = math.prod(lax.axis_size(axis) for axis in axes)
    return lax.ppermute(block, axes, [(i, i + distance) for i in range(size - distance)])


def flip(block, axis):
    return lax.ppermute(block, axis, [(0, 1), (1, 0)])


def local(queries, keys, values, lengths):
    rows = keys.shape[0]
    pair = jnp.stack([keys.reshape(rows, GROUPS, HEAD), values.reshape(rows, GROUPS, HEAD)], 2)
    pair = pair.reshape(rows, GROUPS * 2 * HEAD)
    chain = ("y", "w", "X")
    heads = ("l", "d")
    index, core = lax.axis_index(chain), lax.axis_index("c")
    scalars, lows = bounds(index, core, lengths)
    own = lax.all_to_all(pair, heads, split_axis=1, concat_axis=0, tiled=True)
    q = lax.all_to_all(queries, heads, split_axis=1, concat_axis=0, tiled=True)
    near = jnp.stack([own, forward(own, chain, 2), forward(own, chain, 4)])
    send = lax.dynamic_slice_in_dim(near, lax.axis_index("X"), 2, 0)
    distant = flip(send, "X")
    near_other = flip(near, "c")
    keys = [ready(near, near_other), near, near_other]
    m, acc = fold((0, 1, 2), scalars, q, lows, keys)
    distant, m = lax.optimization_barrier((distant, m))
    keys = [distant, flip(distant, "c")]
    out = fold((3, 4), scalars, q, lows, keys, (m, acc), last=True)
    return lax.all_to_all(out, heads, split_axis=0, concat_axis=1, tiled=True)


def solution(mesh):
    fine = Mesh(mesh.devices.reshape(8, 2, 2, 2, 2, 4), ("y", "w", "X", "l", "c", "d"))
    rows = P(("y", "w", "X", "l", "c", "d"), None)
    return jax.shard_map(
        local, mesh=fine, in_specs=(rows, rows, rows, P()), out_specs=rows, check_vma=False
    )
```

```python
import functools
import math

import jax
import jax.numpy as jnp
from jax import lax
from jax.experimental import pallas as pl
from jax.experimental.pallas import tpu as pltpu
from jax.sharding import Mesh, PartitionSpec as P

HEAD = 128
HEADS = 40
GROUPS = 8
PER_GROUP = HEADS // GROUPS
PART = 256
TILE = 2 * PART
SUPER = 2 * TILE
ROWS = PER_GROUP * PART
SCALE = math.log2(math.e) / math.sqrt(HEAD)
LOWEST = -1e30


def double(x, times=2):
    return jnp.concatenate([x] * times, 1)


def visit(q, kt, v, m_ref, acc_ref, allowed):
    scores = jnp.dot(q, kt, preferred_element_type=jnp.float32)
    weights, decay = [], []
    for head in range(PER_GROUP):
        rows = slice(head * PART, (head + 1) * PART)
        raw = scores[rows]
        if allowed is not None:
            raw = jnp.where(allowed, raw, LOWEST)
        m_old = m_ref[rows]
        m_new = jnp.maximum(m_old, jnp.max(raw, 1, keepdims=True))
        m_ref[rows] = m_new
        decay.append(jnp.exp2((m_old - m_new) * SCALE))
        weights.append(jnp.exp2((raw - double(m_new, TILE // HEAD)) * SCALE).astype(jnp.bfloat16))
    part = jnp.dot(jnp.concatenate(weights, 0), v, preferred_element_type=jnp.float32)
    for head in range(PER_GROUP):
        rows = slice(head * PART, (head + 1) * PART)
        acc_ref[rows] = acc_ref[rows] * double(decay[head]) + part[rows]


def halves(own_refs, other_refs):
    tile = 0
    for own, other in zip(own_refs, other_refs):
        for half in range(2):
            rows = slice(half * PART, (half + 1) * PART)
            for source, ref in enumerate((own, other)):
                yield tile, slice(source * PART, (source + 1) * PART), ref, rows
            tile += 1


def load_keys(own_refs, other_refs, kt_s):
    for tile, span, ref, rows in halves(own_refs, other_refs):
        kt_s[tile, :, span] = ref[rows, :HEAD].T


def load_values(own_refs, other_refs, v_s):
    for tile, span, ref, rows in halves(own_refs, other_refs):
        v_s[tile, span, :HEAD] = ref[rows, HEAD:]
        v_s[tile, span, HEAD:] = jnp.ones((PART, HEAD), jnp.bfloat16)


def sweep(scalars, block, sources, q_s, lows_ref, m_ref, acc_ref):
    first = scalars[block]
    low_first = scalars[2 + block]
    low_last = scalars[4 + block]
    core = scalars[6]
    rows = pl.ds(pl.multiple_of(block * PART, PART), PART)
    for slot, kt_s, key_place, v_s, value_place in sources:
        base = scalars[7 + slot]
        start = jnp.clip((low_first - base) // TILE, 0, 2)
        stop = jnp.clip((first + PART - 1 - base) // TILE + 1, 0, 2)

        def step(tile, _):
            position = base + tile * TILE
            whole = (position >= low_last) & (position + TILE - 1 <= first)

            def go(allowed):
                kt, v = kt_s[key_place + tile], v_s[value_place + tile]
                visit(q_s[block], kt, v, m_ref.at[block], acc_ref.at[block], allowed)

            @pl.when(whole)
            def _():
                go(None)

            @pl.when(jnp.logical_not(whole))
            def _():
                column = lax.broadcasted_iota(jnp.int32, (PART, TILE), 1)
                key = position + jnp.bitwise_xor(column, core * PART)
                query = first + lax.broadcasted_iota(jnp.int32, (PART, TILE), 0)
                low = double(lows_ref[rows, :], TILE // HEAD)
                go((key <= query) & (key >= low))

            return 0

        lax.fori_loop(start, stop, step, 0)


def stack_heads(q_ref, q_s):
    for block in range(2):
        for head in range(PER_GROUP):
            q_s[block, head * PART : (head + 1) * PART] = q_ref[
                block * PART : (block + 1) * PART, head * HEAD : (head + 1) * HEAD
            ]


def blocks(ref):
    return [ref.at[i] for i in range(ref.shape[0])]


def ready_kernel(own, other, kt_ref):
    load_keys(blocks(own), blocks(other), kt_ref)


def ready(own, other):
    vmem = pl.BlockSpec(memory_space=pltpu.VMEM)
    return pl.pallas_call(
        ready_kernel,
        out_shape=jax.ShapeDtypeStruct((2 * own.shape[0], HEAD, TILE), jnp.bfloat16),
        in_specs=[vmem] * 2,
        out_specs=vmem,
        compiler_params=PARAMS,
        cost_estimate=cost(8),
        name="ready",
    )(own, other)


def fold_kernel(slots, first, last, scalars, q_ref, lows_ref, *refs):
    if first:
        kt_ref, own, other, own_last, other_last, m_ref, acc_ref, q_s, kt_s, v_s = refs
        load_keys([own_last], [other_last], kt_s)
        load_values(blocks(own) + [own_last], blocks(other) + [other_last], v_s)
        sources = [(slot, kt_ref, 2 * i, v_s, 2 * i) for i, slot in enumerate(slots[:-1])]
        sources.append((slots[-1], kt_s, 0, v_s, 2 * len(sources)))
        m_ref[...] = jnp.full(m_ref.shape, LOWEST, jnp.float32)
        acc_ref[...] = jnp.zeros(acc_ref.shape, jnp.float32)
    else:
        own, other, m_in, acc_in, out_ref, m_ref, acc_ref, q_s, kt_s, v_s = refs
        load_keys(blocks(own), blocks(other), kt_s)
        load_values(blocks(own), blocks(other), v_s)
        sources = [(slot, kt_s, 2 * i, v_s, 2 * i) for i, slot in enumerate(slots)]
        m_ref[...] = m_in[...]
        acc_ref[...] = acc_in[...]
    stack_heads(q_ref, q_s)

    def one(block, _):
        sweep(scalars, block, sources, q_s, lows_ref, m_ref, acc_ref)
        if last:
            rows = pl.ds(pl.multiple_of(block * PART, PART), PART)
            for head in range(PER_GROUP):
                total = acc_ref[block, head * PART : (head + 1) * PART]
                out_ref[rows, head * HEAD : (head + 1) * HEAD] = (
                    total[:, :HEAD] / total[:, HEAD:]
                ).astype(jnp.bfloat16)
        return 0

    lax.fori_loop(0, 2, one, 0)


def specs(count):
    return [pl.BlockSpec(memory_space=pltpu.SMEM)] + [pl.BlockSpec(memory_space=pltpu.VMEM)] * count


def scratch(tiles):
    return [
        pltpu.VMEM((2, ROWS, HEAD), jnp.bfloat16),
        pltpu.VMEM((tiles, HEAD, TILE), jnp.bfloat16),
        pltpu.VMEM((tiles, TILE, 2 * HEAD), jnp.bfloat16),
    ]


def cost(tiles):
    pairs = 2 * ROWS * tiles * TILE
    return pl.CostEstimate(flops=4 * HEAD * pairs, bytes_accessed=4 << 20, transcendentals=pairs)


STATE = (
    jax.ShapeDtypeStruct((2, ROWS, HEAD), jnp.float32),
    jax.ShapeDtypeStruct((2, ROWS, 2 * HEAD), jnp.float32),
)
PARAMS = pltpu.CompilerParams(vmem_limit_bytes=32 * 1024 * 1024)


def fold(slots, scalars, q, lows, keys, state=(), last=False):
    vmem = pl.BlockSpec(memory_space=pltpu.VMEM)
    keep = [pltpu.VMEM(s.shape, s.dtype) for s in STATE] if last else []
    return pl.pallas_call(
        functools.partial(fold_kernel, slots, not state, last),
        out_shape=jax.ShapeDtypeStruct(q.shape, jnp.bfloat16) if last else STATE,
        in_specs=specs(2 + len(keys) + len(state)),
        out_specs=vmem if last else [vmem] * 2,
        scratch_shapes=keep + scratch(2 * len(slots)),
        compiler_params=PARAMS,
        cost_estimate=cost(2 * len(slots)),
        name="attend_%d" % slots[0],
    )(scalars, q, lows, *keys, *state)


def pack_kernel(keys_ref, values_ref, out_ref):
    for group in range(GROUPS):
        columns = slice(group * HEAD, (group + 1) * HEAD)
        out_ref[group, :, :HEAD] = keys_ref[:, columns]
        out_ref[group, :, HEAD:] = values_ref[:, columns]


def pack(keys, values):
    vmem = pl.BlockSpec(memory_space=pltpu.VMEM)
    return pl.pallas_call(
        pack_kernel,
        out_shape=jax.ShapeDtypeStruct((GROUPS, keys.shape[0], 2 * HEAD), jnp.bfloat16),
        in_specs=[vmem] * 2,
        out_specs=vmem,
        cost_estimate=pl.CostEstimate(flops=0, bytes_accessed=1 << 19, transcendentals=0),
        name="pack",
    )(keys, values)


def bounds(index, core, lengths):
    starts = jnp.cumsum(lengths) - lengths
    firsts = index * SUPER + core * PART + jnp.arange(2, dtype=jnp.int32) * TILE
    query = (firsts[:, None] + jnp.arange(PART, dtype=jnp.int32)[None, :]).reshape(TILE)
    low = jnp.max(jnp.where(starts[None, :] <= query[:, None], starts[None, :], 0), 1)
    lows = jnp.broadcast_to(low[:, None], (TILE, HEAD))
    bases = [index, index - 2, index - 4, index - 1, index - 3]
    place = jnp.stack([core] + [base * SUPER for base in bases])
    scalars = jnp.concatenate([firsts, low[::PART], low[PART - 1 :: PART], place])
    return scalars.astype(jnp.int32), lows.astype(jnp.int32)


def forward(block, axes, distance):
    size = math.prod(lax.axis_size(axis) for axis in axes)
    return lax.ppermute(block, axes, [(i, i + distance) for i in range(size - distance)])


def flip(block, axis):
    return lax.ppermute(block, axis, [(0, 1), (1, 0)])


def local(queries, keys, values, lengths):
    rows = keys.shape[0]
    chain = ("y", "w", "X")
    heads = ("l", "d")
    index, core = lax.axis_index(chain), lax.axis_index("c")
    scalars, lows = bounds(index, core, lengths)
    own = lax.all_to_all(pack(keys, values), heads, split_axis=0, concat_axis=0, tiled=True)
    asked = queries.reshape(rows, GROUPS, PER_GROUP * HEAD).transpose(1, 0, 2)
    own, asked = lax.optimization_barrier((own, asked))
    own = own.reshape(GROUPS * rows, 2 * HEAD)
    q = lax.all_to_all(asked, heads, split_axis=0, concat_axis=0, tiled=True)
    q = q.reshape(GROUPS * rows, PER_GROUP * HEAD)
    two = forward(own, chain, 2)
    four = forward(own, chain, 4)
    near = jnp.stack([own, two])
    left = lax.axis_index("X") == 0
    mine, nearby, farther = lax.optimization_barrier((own, two, four))
    send = jnp.stack([jnp.where(left, mine, nearby), jnp.where(left, nearby, farther)])
    distant = flip(send, "X")
    near_other = flip(near, "c")
    keys = [ready(near, near_other), near, near_other, four, flip(four, "c")]
    m, acc = fold((0, 1, 2), scalars, q, lows, keys)
    distant, m = lax.optimization_barrier((distant, m))
    keys = [distant, flip(distant, "c")]
    out = fold((3, 4), scalars, q, lows, keys, (m, acc), last=True)
    return lax.all_to_all(out, heads, split_axis=0, concat_axis=1, tiled=True)


def solution(mesh):
    fine = Mesh(mesh.devices.reshape(8, 2, 2, 2, 2, 4), ("y", "w", "X", "l", "c", "d"))
    rows = P(("y", "w", "X", "l", "c", "d"), None)
    return jax.shard_map(
        local, mesh=fine, in_specs=(rows, rows, rows, P()), out_specs=rows, check_vma=False
    )
```
